256 devices in a mesh: tm: 64 (over y, x_hi, z), mode: 4 (over x_lo, core).
Axes of the slice: x: 4 (x_hi: 2, x_lo: 2; x = x_hi * 2 + x_lo), y: 4, z: 8, core: 2. Of those that a mesh axis runs over, the one named last changes fastest.
Arguments:
- fields_left: bfloat16 [2, 2, 64, 1024, 1024], P(None, None, 'tm', 'mode'), may hold values from -0.125 to 0.125
- fields_right: bfloat16 [2, 2, 64, 1024, 1024], P(None, None, 'tm', 'mode'), may hold values from -6 to 6
- delta: int32 [2], replicated, may hold values from 1 to 7, as said below
- pair: int32 [2], replicated, may hold values from 0 to 1, each once
Outputs:
- rectangle: float32 [64, 2, 2, 2, 6], P('tm')
- box: float32 [64, 2, 2, 2, 6], P('tm')
The draws below stay inside these ranges and needn't reach their ends.
Inputs may be any that keep to these rules, and one draw needn't show every extreme that they name: `delta`: the offsets are distinct, and exactly one of them is 7. Each momentum pair is used by exactly one product.
All inputs are finite; a program needn't handle non-finite values.
Results may differ from the reference program's by a relative error of at most 0.004.
Values may be sent and summed in bfloat16 or wider, within the bound.
A program may use at most 128 MiB of HBM per device.

```python
import jax
import jax.numpy as jnp
from jax import lax

N = 1024
Q = 2
HALF = 3
DMAX = 7
TS = 64


def draw_delta(key, part):
    key = jax.random.fold_in(key, 7)
    first_key, second_key = jax.random.split(key)
    others = jax.random.permutation(first_key, DMAX - 1)[:Q - 1] + 1
    values = jnp.concatenate([others, jnp.array([DMAX], jnp.int32)]).astype(jnp.int32)
    placing = jax.random.permutation(second_key, Q)
    return values[placing].astype(jnp.int32)


def block_levels(own_key, extent, pieces, low, top_value):
    loudness, own = 1.0, jax.random.fold_in(own_key, 6)
    for dim, shards_of in pieces:
        heights = jnp.exp(jax.random.uniform(jax.random.fold_in(own, dim), (shards_of,), jnp.float32, low / len(pieces), top_value / len(pieces)))
        loudness = loudness * jnp.repeat(heights, extent[dim] // shards_of).reshape([-1 if axis == dim else 1 for axis in range(len(extent))])
    return loudness


def gaussian(key, extent, scale, limit, shards=(), held_as=jnp.bfloat16):
    values = scale * jax.random.normal(key, extent, jnp.float32)
    if shards:
        values = values * block_levels(key, extent, shards, -0.22, 0.18)
    return jnp.clip(values, -limit, limit).astype(held_as)


def setup_inputs(seed: int = 0) -> dict:
    streams_of = jax.random.split(jax.random.key(seed), 5)
    fields_left = gaussian(streams_of[0], (Q, 2, TS, N, N), (2 * N) ** -0.5, 0.125, ((2, 64), (3, 4)))
    fields_right = gaussian(streams_of[1], (Q, 2, TS, N, N), 1.0, 6.0, ((2, 64), (3, 4)))
    delta = draw_delta(jax.random.fold_in(streams_of[4], 71), 0)
    pair = jax.random.permutation(streams_of[3], Q).astype(jnp.int32)
    return dict(fields_left=fields_left, fields_right=fields_right, delta=delta, pair=pair)


def reference(fields_left, fields_right, delta, pair):
    total_time = fields_left.shape[2]
    width = fields_left.shape[3]
    count = delta.shape[0]

    def make_products(time_index):
        result = []
        for product_index in range(count):
            left_field = fields_left[pair[product_index], :, time_index]
            later = (time_index + delta[product_index]) % total_time
            right_field = fields_right[pair[product_index], :, later]
            real_part = jnp.dot(left_field[0], right_field[0], preferred_element_type=jnp.float32) - jnp.dot(left_field[1], right_field[1], preferred_element_type=jnp.float32)
            imag_part = jnp.dot(left_field[0], right_field[1], preferred_element_type=jnp.float32) + jnp.dot(left_field[1], right_field[0], preferred_element_type=jnp.float32)
            result.append(jnp.stack([real_part, imag_part]))
        return jnp.stack(result).astype(jnp.bfloat16)

    products = lax.map(make_products, jnp.arange(total_time, dtype=jnp.int32))
    traces = jnp.sum(jnp.diagonal(products, axis1=3, axis2=4).astype(jnp.float32), axis=-1)

    def correlate(time_index):
        source = products[time_index].astype(jnp.float32)
        columns = []
        for sep_index in range(1, 2 * HALF + 1):
            sink = products[(time_index + sep_index) % total_time].astype(jnp.float32)
            real_part = jnp.einsum('kcij,lcij->kl', source, sink)
            imag_part = jnp.einsum('kij,lij->kl', source[:, 1], sink[:, 0]) - jnp.einsum('kij,lij->kl', source[:, 0], sink[:, 1])
            columns.append(jnp.stack([real_part, imag_part]))
        return jnp.stack(columns, axis=-1)

    rectangle = lax.map(correlate, jnp.arange(total_time, dtype=jnp.int32)) / width
    times = jnp.arange(total_time, dtype=jnp.int32)
    separations = jnp.arange(1, 2 * HALF + 1, dtype=jnp.int32)
    later = traces[(times[:, None] + separations[None, :]) % total_time]
    here = traces
    box_real = here[:, :, None, None, 0] * later[:, None, :, :, 0].transpose(0, 1, 3, 2) + here[:, :, None, None, 1] * later[:, None, :, :, 1].transpose(0, 1, 3, 2)
    box_imag = here[:, :, None, None, 1] * later[:, None, :, :, 0].transpose(0, 1, 3, 2) - here[:, :, None, None, 0] * later[:, None, :, :, 1].transpose(0, 1, 3, 2)
    box = jnp.stack([box_real, box_imag], axis=1) / width
    return rectangle, box
```

```python
import functools

import jax
import jax.numpy as jnp
from jax import lax
from jax.experimental import pallas as pl
from jax.experimental.pallas import tpu as pltpu
from jax.sharding import PartitionSpec as P

HALF = 3
DMAX = 7
MESH = pl.DeviceIdType.MESH
DMA = pltpu.SemaphoreType.DMA
T = 64
RING = 8
ROWS = 256
N = 1024
CHUNKS = 4
WIDE = N // CHUNKS
STEPS = 2 * CHUNKS
MIB = 2**20


def remote(src, dst, send, recv, device):
    return pltpu.make_async_remote_copy(
        src_ref=src, dst_ref=dst, send_sem=send, recv_sem=recv, device_id=device, device_id_type=MESH
    )


def greet(devices):
    barrier = pltpu.get_barrier_semaphore()
    for device in devices:
        pl.semaphore_signal(barrier, inc=1, device_id=device, device_id_type=MESH)
    pl.semaphore_wait(barrier, len(devices))


def meet_kernel(
    offset, first_ref, left_ref, right_ref, out_ref, sent, whole, s1, r1, s2, r2, s3, r3, s4, r4
):
    t, m = lax.axis_index("tm"), lax.axis_index("mode")
    across = (t, lax.rem(m + 2, 4))
    core = (t, m + 1 - 2 * lax.rem(m, 2))
    targets, sources = [], []
    for shift in (DMAX, offset):
        later, earlier = lax.rem(t + shift, T), lax.rem(t + T - shift, T)
        flip_in = lax.rem(t // RING + later // RING, 2)
        flip_out = lax.rem(t // RING + earlier // RING, 2)
        sources.append((later, lax.rem(m + 2 * flip_in, 4)))
        targets.append((earlier, lax.rem(m + 2 * flip_out, 4)))
    greet([sources[0], sources[1], across, core])

    first = first_ref[0]

    def field(product):
        return first if product == 0 else 1 - first

    def rows_of(mode):
        return pl.ds(pl.multiple_of(mode * ROWS, ROWS), ROWS)

    def block(step, mode):
        return whole.at[step, :, rows_of(mode), :]

    def shifted(step, product):
        return remote(sent.at[step], block(step, m), s1.at[step], r1.at[step], targets[product])

    def over_chips(step, product):
        part = block(step, sources[product][1])
        return remote(part, part, s2.at[step], r2.at[step], across)

    def over_cores(step, product):
        part = block(step, sources[product][1])
        return remote(part, part, s3.at[step], r3.at[step], core)

    def over_cores_late(step, product):
        part = block(step, lax.rem(sources[product][1] + 2, 4))
        return remote(part, part, s4.at[step], r4.at[step], core)

    for step in range(STEPS):
        product, column = step % 2, step // 2
        sent[step] = right_ref[field(product), :, :, column * WIDE : (column + 1) * WIDE]
        shifted(step, product).start()

    def multiply(column, product):
        step = 2 * column + product
        over_cores(step, product).wait_recv()
        over_cores_late(step, product).wait_recv()
        real_left, imag_left = left_ref[field(product), 0], left_ref[field(product), 1]
        real_right, imag_right = whole[step, 0], whole[step, 1]
        dot = functools.partial(jnp.dot, preferred_element_type=jnp.float32)
        real = dot(real_left, real_right) - dot(imag_left, imag_right)
        imag = dot(real_left, imag_right) + dot(imag_left, real_right)
        pieces = jnp.concatenate(
            [real.reshape(ROWS // 8, 8, WIDE), imag.reshape(ROWS // 8, 8, WIDE)], axis=1
        ).astype(jnp.bfloat16)
        place = pl.ds(pl.multiple_of((column // 2) * 32, 32), 32)
        lanes = pl.ds(pl.multiple_of(lax.rem(column, 2) * WIDE, WIDE), WIDE)
        out_ref[product, place, :, lanes] = pieces

    def turn(i, _):
        @pl.when(i < CHUNKS)
        def _():
            for product in range(2):
                shifted(2 * i + product, product).wait_recv()
                over_chips(2 * i + product, product).start()
                over_cores(2 * i + product, product).start()

        @pl.when((i >= 1) & (i < CHUNKS + 1))
        def _():
            for product in range(2):
                over_chips(2 * (i - 1) + product, product).wait_recv()
                over_cores_late(2 * (i - 1) + product, product).start()

        @pl.when(i >= 2)
        def _():
            for product in range(2):
                multiply(i - 2, product)

        return 0

    lax.fori_loop(0, CHUNKS + 2, turn, 0)

    def finish(i, _):
        for product in range(2):
            for copy in (shifted, over_chips, over_cores, over_cores_late):
                copy(2 * i + product, product).wait_send()
        return 0

    lax.fori_loop(0, CHUNKS, finish, 0)


def meet(offset, collective, first, left, right):
    vmem = pl.BlockSpec(memory_space=pltpu.VMEM)
    return pl.pallas_call(
        functools.partial(meet_kernel, offset),
        out_shape=jax.ShapeDtypeStruct((2, T, 16, 512), jnp.bfloat16),
        in_specs=[pl.BlockSpec(memory_space=pltpu.SMEM), vmem, vmem],
        out_specs=vmem,
        scratch_shapes=[
            pltpu.VMEM((STEPS, 2, ROWS, WIDE), jnp.bfloat16),
            pltpu.VMEM((STEPS, 2, N, WIDE), jnp.bfloat16),
        ]
        + [DMA((STEPS,))] * 8,
        compiler_params=pltpu.CompilerParams(
            collective_id=collective, has_side_effects=True, vmem_limit_bytes=48 * MIB
        ),
    )(first, left, right)


def spread_lanes(value):
    row = lax.broadcasted_iota(jnp.int32, value.shape, 0)
    for bit in range(6):
        use = lax.rem(row // (1 << bit), 2) == 1
        value = jnp.where(use, pltpu.roll(value, 128 - (2 << bit), 1), value)
    return value


def gram_kernel(
    in_ref, out_ref, got, wide, part_a, part_b, part_c, own, sa, ra, sb, rb, sc, rc, sd, rd
):
    t, m = lax.axis_index("tm"), lax.axis_index("mode")
    z, ring = lax.rem(t, RING), t // RING
    barrier = pltpu.get_barrier_semaphore()

    def hello(i, _):
        pl.semaphore_signal(
            barrier, inc=1, device_id=(lax.rem(t + i, T), m), device_id_type=MESH
        )
        return 0

    lax.fori_loop(1, T, hello, 0)
    for i in range(1, 4):
        pl.semaphore_signal(
            barrier, inc=1, device_id=(t, lax.rem(m + i, 4)), device_id_type=MESH
        )
    pl.semaphore_wait(barrier, T - 1 + 3)

    def send(i, _):
        odd = lax.rem(i, 2)
        ahead = odd * ((i + 1) // 2) + (1 - odd) * (T - i // 2)
        to = lax.rem(t + ahead, T)
        remote(in_ref.at[:, to], got.at[:, t], sa, ra, (to, m)).start()
        return 0

    lax.fori_loop(1, T, send, 0)
    got[:, t] = in_ref[:, t]
    remote(in_ref.at[:, pl.ds(0, T - 1)], got.at[:, pl.ds(0, T - 1)], sa, ra, (lax.rem(t + 1, T), m)).wait()

    rows = 2 * T * 16
    for j in range(4):
        piece = got[:, :, :, j * 128 : (j + 1) * 128].astype(jnp.float32)
        wide[pl.ds(j * rows, rows), :] = piece.reshape(rows, 128)

    def strided(start, count, stride):
        pieces = [wide[pl.ds(j * rows + start, count, stride=stride), :] for j in range(4)]
        return jnp.concatenate(pieces, axis=1).astype(jnp.bfloat16)

    lane = lax.broadcasted_iota(jnp.int32, (16, 512), 1) + (t // 32) * 512
    grams = jnp.zeros((256, 256), jnp.float32)
    traces = jnp.zeros((16, 256), jnp.float32)
    for r in range(8):
        right = strided(r, 256, 8)
        left = jnp.concatenate([strided(r, 128, 16), strided(r + 8, 128, 16)], axis=0)
        diagonal = jnp.where(lane == m * ROWS + lax.rem(t, 32) * 8 + r, 1.0, 0.0).astype(jnp.bfloat16)
        over_lanes = (((1,), (1,)), ((), ()))
        grams += lax.dot_general(left, right, over_lanes, preferred_element_type=jnp.float32)
        traces += lax.dot_general(diagonal, right, over_lanes, preferred_element_type=jnp.float32)

    place = lax.broadcasted_iota(jnp.int32, (T, 128), 1) // 16
    packed = jnp.zeros((T, 128), jnp.float32)
    packed_traces = jnp.zeros((T, 128), jnp.float32)
    for c in range(2):
        for p in range(2):
            for l in range(2):
                index = c * 4 + p * 2 + l
                top = c * 128 + p * 64
                value = spread_lanes(grams[top : top + 64, l * 128 : (l + 1) * 128])
                value = pltpu.roll(value, 16 * index, 1) if index else value
                packed = jnp.where(place == index, value, packed)
    for l in range(2):
        value = jnp.broadcast_to(traces[0:1, l * 128 : (l + 1) * 128], (T, 128))
        value = spread_lanes(value)
        value = pltpu.roll(value, 16 * l, 1) if l else value
        packed_traces = jnp.where(place == l, value, packed_traces)
    own[:, :, 0:128] = packed.reshape(8, 8, 128)
    own[:, :, 128:256] = packed_traces.reshape(8, 8, 128)

    copies = []
    for i in range(1, 8):
        to = lax.rem(ring + i, 8)
        copies.append(remote(own.at[to], part_a.at[ring], sb.at[i], rb.at[i], (to * RING + z, m)))
    for copy in copies:
        copy.start()
    part_a[ring] = own[ring]
    for copy in copies:
        copy.wait()
    own[0] = jnp.sum(part_a[...], axis=0)

    copies = []
    for i in range(1, 8):
        to = lax.rem(z + i, 8)
        copies.append(remote(own.at[0], part_b.at[z], sc.at[i], rc.at[i], (ring * RING + to, m)))
    for copy in copies:
        copy.start()
    part_b[z] = own[0]
    for copy in copies:
        copy.wait()
    own[1] = jnp.sum(part_b[...], axis=0)

    copies = []
    for i in range(1, 4):
        to = lax.rem(m + i, 4)
        copies.append(remote(own.at[1], part_c.at[m], sd.at[i], rd.at[i], (t, to)))
    for copy in copies:
        copy.start()
    part_c[m] = own[1]
    for copy in copies:
        copy.wait()
    out_ref[...] = part_c[0] + part_c[1] + part_c[2] + part_c[3]


def gram(products):
    vmem = pl.BlockSpec(memory_space=pltpu.VMEM)
    return pl.pallas_call(
        gram_kernel,
        out_shape=jax.ShapeDtypeStruct((8, 256), jnp.float32),
        in_specs=[vmem],
        out_specs=vmem,
        scratch_shapes=[
            pltpu.VMEM((2, T, 16, 512), jnp.bfloat16),
            pltpu.VMEM((4 * 2 * T * 16, 128), jnp.float32),
            pltpu.VMEM((8, 8, 256), jnp.float32),
            pltpu.VMEM((8, 8, 256), jnp.float32),
            pltpu.VMEM((4, 8, 256), jnp.float32),
            pltpu.VMEM((8, 8, 256), jnp.float32),
            DMA, DMA, DMA((8,)), DMA((8,)), DMA((8,)), DMA((8,)), DMA((4,)), DMA((4,)),
        ],
        compiler_params=pltpu.CompilerParams(
            collective_id=0, has_side_effects=True, vmem_limit_bytes=48 * MIB
        ),
    )(products)


def on_device(fields_left, fields_right, delta, pair):
    left, right = fields_left[:, :, 0], fields_right[:, :, 0]
    largest = jnp.argmax(delta).astype(jnp.int32)
    first = pair[largest].reshape(1)
    other = delta[1 - largest]
    branches = [functools.partial(meet, offset, offset) for offset in range(1, DMAX)]
    products = lax.switch(other - 1, branches, first, left, right)
    sums = gram(products)
    z = lax.rem(lax.axis_index("tm"), RING)
    row = lax.dynamic_slice_in_dim(sums, z, 1, 0)[0]
    order = jnp.where(jnp.arange(2) == largest, 0, 1)
    grams = row[:128].reshape(2, 2, 2, 8, 2)
    grams = grams[:, :, :, 1:7][:, order][:, :, order]
    rect_real = grams[0, ..., 0] + grams[1, ..., 1]
    rect_imag = grams[1, ..., 0] - grams[0, ..., 1]
    traces = row[128:160].reshape(2, 8, 2)[order]
    here = traces[:, 0][:, None, None, :]
    there = traces[:, 1:7][None]
    box_real = here[..., 0] * there[..., 0] + here[..., 1] * there[..., 1]
    box_imag = here[..., 1] * there[..., 0] - here[..., 0] * there[..., 1]
    rectangle = jnp.stack([rect_real, rect_imag]) / N
    box = jnp.stack([box_real, box_imag]) / N
    return rectangle[None], box[None]


def solution(mesh):
    split = P(None, None, "tm", "mode", None)
    out = P("tm", None, None, None, None)
    return jax.shard_map(
        on_device, mesh=mesh, in_specs=(split, split, P(), P()), out_specs=(out, out), check_vma=False
    )
```

```python
import functools

import jax
import jax.numpy as jnp
from jax import lax
from jax.experimental import pallas as pl
from jax.experimental.pallas import tpu as pltpu
from jax.sharding import PartitionSpec as P

HALF = 3
DMAX = 7
MESH = pl.DeviceIdType.MESH
DMA = pltpu.SemaphoreType.DMA
T = 64
RING = 8
ROWS = 256
N = 1024
CHUNKS = 4
WIDE = N // CHUNKS
STEPS = 2 * CHUNKS
MIB = 2**20


def remote(src, dst, send, recv, device):
    return pltpu.make_async_remote_copy(
        src_ref=src, dst_ref=dst, send_sem=send, recv_sem=recv, device_id=device, device_id_type=MESH
    )


def rolled_rows(value):
    row = lax.broadcasted_iota(jnp.int32, value.shape, 0)
    for bit in range(6):
        use = lax.rem(row // (1 << bit), 2) == 1
        value = jnp.where(use, pltpu.roll(value, 128 - (2 << bit), 1), value)
    return value


def lanes_of(shape, axis):
    return lax.broadcasted_iota(jnp.int32, shape, axis)


def fused_kernel(
    offset, ahead, delta_ref, pair_ref, left_ref, right_ref, out_ref,
    left_in, right_in, left_op, left_sent, sent, whole, made, got, wide, folded, grams, picks,
    own, part_a, part_b, part_c, last,
    in_sem, sl, rl, s1, r1, s2, r2, s3, r3, s4, r4, sa, ra, sb, rb, sc, rc, sd, rd,
):
    t, m = lax.axis_index("tm"), lax.axis_index("mode")
    z, ring = lax.rem(t, RING), t // RING
    moves = (DMAX, (offset - ahead) % T)
    loads = [
        pltpu.make_async_copy(right_ref, right_in, in_sem.at[0]),
        pltpu.make_async_copy(left_ref, left_in, in_sem.at[1]),
    ]
    for load in loads:
        load.start()

    across = (t, lax.rem(m + 2, 4))
    core = (t, m + 1 - 2 * lax.rem(m, 2))
    targets, sources = [], []
    for shift in moves:
        later, earlier = lax.rem(t + shift, T), lax.rem(t + T - shift, T)
        flip_in = lax.rem(t // RING + later // RING, 2)
        flip_out = lax.rem(t // RING + earlier // RING, 2)
        sources.append((later, lax.rem(m + 2 * flip_in, 4)))
        targets.append((earlier, lax.rem(m + 2 * flip_out, 4)))

    barrier = pltpu.get_barrier_semaphore()

    def hello(i, _):
        pl.semaphore_signal(barrier, inc=1, device_id=(lax.rem(t + i, T), m), device_id_type=MESH)
        return 0

    for source in sources:
        pl.semaphore_signal(barrier, inc=1, device_id=source, device_id_type=MESH)
    for i in range(1, 4):
        pl.semaphore_signal(barrier, inc=1, device_id=(t, lax.rem(m + i, 4)), device_id_type=MESH)
    lax.fori_loop(1, T, hello, 0)

    in_order = delta_ref[0] == DMAX
    first = jnp.where(in_order, pair_ref[0], pair_ref[1])

    loads[0].wait()
    for product in range(2):
        field = first if product == 0 else 1 - first
        for column in range(CHUNKS):
            sent[product * CHUNKS + column] = right_in[field, :, :, column * WIDE : (column + 1) * WIDE]
    pl.semaphore_wait(barrier, T - 1 + 3 + 2)

    source_modes = (sources[0][1], sources[1][1])

    def block(step, mode):
        return whole.at[step, :, pl.ds(pl.multiple_of(mode * ROWS, ROWS), ROWS), :]

    def shifted(step, product):
        return remote(sent.at[step], block(step, m), s1.at[step], r1.at[step], targets[product])

    def source_mode(step):
        product = step // CHUNKS
        return source_modes[0] * (1 - product) + source_modes[1] * product

    def over_chips(step):
        part = block(step, source_mode(step))
        return remote(part, part, s2.at[step], r2.at[step], across)

    def over_cores(step):
        part = block(step, source_mode(step))
        return remote(part, part, s3.at[step], r3.at[step], core)

    def over_cores_late(step):
        part = block(step, lax.rem(source_mode(step) + 2, 4))
        return remote(part, part, s4.at[step], r4.at[step], core)

    for column in range(CHUNKS):
        for product in range(2):
            shifted(product * CHUNKS + column, product).start()

    loads[1].wait()
    left_op[0] = left_in[first]
    if ahead == 0:
        left_op[1] = left_in[1 - first]
    else:
        left_sent[...] = left_in[1 - first]
        left_move = remote(left_sent, left_op.at[1], sl, rl, (lax.rem(t + ahead + T, T), m))
        left_move.start()

    def multiply(step):
        product, column = step // CHUNKS, lax.rem(step, CHUNKS)
        over_cores(step).wait_recv()
        over_cores_late(step).wait_recv()
        real_left, imag_left = left_op[product, 0], left_op[product, 1]
        real_right, imag_right = whole[step, 0], whole[step, 1]
        dot = functools.partial(jnp.dot, preferred_element_type=jnp.float32)
        real = dot(real_left, real_right) - dot(imag_left, imag_right)
        imag = dot(real_left, imag_right) + dot(imag_left, real_right)
        pieces = jnp.concatenate(
            [real.reshape(ROWS // 8, 8, WIDE), imag.reshape(ROWS // 8, 8, WIDE)], axis=1
        ).astype(jnp.bfloat16)
        place = pl.ds(pl.multiple_of(lax.rem(column, 2) * 32, 32), 32)
        made[product, column // 2, place] = pieces

    def spread(product, half):
        slot = lax.rem(t + T - ahead * product, T)

        def send(i, _):
            odd = lax.rem(i, 2)
            far = odd * ((i + 1) // 2) + (1 - odd) * (T - i // 2)
            to = lax.rem(t + far, T)
            remote(
                made.at[product, half, to], got.at[product, half, slot],
                sa.at[product, half], ra.at[product, half], (to, m),
            ).start()
            return 0

        lax.fori_loop(1, T, send, 0)
        got[product, half, slot] = made[product, half, t]

    def step_at(turn):
        return turn - turn // 5

    def busy(turn):
        return (turn >= 0) & (turn != 4) & (turn < 9)

    def turn_of(i, _):
        @pl.when(busy(i - 2))
        def _():
            step = step_at(i - 2)
            if ahead != 0:
                @pl.when(step == CHUNKS)
                def _():
                    left_move.wait_recv()
            multiply(step)

            @pl.when(lax.rem(step, 2) == 1)
            def _():
                spread(step // CHUNKS, lax.rem(step, CHUNKS) // 2)

        @pl.when(busy(i - 1))
        def _():
            step = step_at(i - 1)
            over_chips(step).wait_recv()
            over_cores_late(step).start()

        @pl.when(busy(i))
        def _():
            step = step_at(i)
            shifted(step, 0).wait_recv()
            over_chips(step).start()
            over_cores(step).start()

        return 0

    lax.fori_loop(0, 11, turn_of, 0)

    sum_row, lane = lanes_of((256, 128), 0), lanes_of((256, 128), 1)
    part, k, l, s = lane // 24, lax.rem(lane // 12, 2), lax.rem(lane // 6, 2), lax.rem(lane, 6) + 1
    swap = jnp.where(in_order, 0, 1)
    k, l = k + swap - 2 * swap * k, l + swap - 2 * swap * l
    valid = lane < 48

    def pick(index, *terms):
        value = jnp.zeros((256, 128), jnp.float32)
        for where, sign in terms:
            value = value + jnp.where((sum_row == where) & valid, sign, 0.0)
        picks[index] = value

    pair_at = (2 * k + l) * 16 + 2 * s
    sign = jnp.where(part == 0, 1.0, -1.0)
    pick(0, (pair_at + 64 * part, 1.0), (pair_at + 1 + 64 * (1 - part), sign))
    for d in range(2):
        pick(1 + d, (128 + k * 16 + d, 1.0))
        pick(3 + d, (128 + l * 16 + 2 * s + d, 1.0))

    over_lanes = (((1,), (1,)), ((), ()))

    def dot_t(a, b):
        return lax.dot_general(a, b, over_lanes, preferred_element_type=jnp.float32)

    mask_lane = lanes_of((16, WIDE), 1)
    traces = [jnp.zeros((16, 128), jnp.float32) for _ in range(2)]

    def absorb(product, half):
        remote(
            made.at[product, half, pl.ds(0, T - 1)], got.at[product, half, pl.ds(0, T - 1)],
            sa.at[product, half], ra.at[product, half], across,
        ).wait()
        count = T * 16
        for j in range(2):
            piece = got[product, half, :, :, j * 128 : (j + 1) * 128].astype(jnp.float32)
            wide[pl.ds(j * count, count), :] = piece.reshape(count, 128)
        for r in range(8):
            pieces = [wide[pl.ds(j * count + r, 128, stride=8), :] for j in range(2)]
            value = jnp.concatenate(pieces, axis=1).astype(jnp.bfloat16)
            folded[product, half, r] = value
            at = (2 * half + t // 32) * WIDE
            hit = mask_lane + at == m * ROWS + lax.rem(t, 32) * 8 + r
            diagonal = jnp.where(hit, 1.0, 0.0).astype(jnp.bfloat16)
            traces[product] += dot_t(diagonal, value)

    def gram(a, b, half):
        value = jnp.zeros((128, 128), jnp.float32)
        for r in range(8):
            value += dot_t(folded[a, half, r], folded[b, half, r])
        return value

    place = lanes_of((T, 128), 1) // 16

    def fold(a, b, packed):
        for c in range(2):
            index = c * 4 + a * 2 + b
            value = rolled_rows(grams[pl.ds((2 * a + b) * 128 + c, T, stride=2), :])
            value = pltpu.roll(value, 16 * index, 1) if index else value
            packed = jnp.where(place == index, value, packed)
        return packed

    def fold_traces(a, packed):
        value = rolled_rows(jnp.broadcast_to(traces[a][0:1], (T, 128)))
        value = pltpu.roll(value, 16 * a, 1) if a else value
        return jnp.where(place == a, value, packed)

    packed = jnp.zeros((T, 128), jnp.float32)
    packed_traces = jnp.zeros((T, 128), jnp.float32)
    absorb(0, 0)
    grams[0:128, :] = gram(0, 0, 0)
    absorb(0, 1)
    grams[0:128, :] += gram(0, 0, 1)
    packed = fold(0, 0, packed)
    packed_traces = fold_traces(0, packed_traces)
    rest = ((0, 1), (1, 0), (1, 1))
    absorb(1, 0)
    for a, b in rest:
        grams[(2 * a + b) * 128 : (2 * a + b + 1) * 128, :] = gram(a, b, 0)
    absorb(1, 1)
    for a, b in rest:
        grams[(2 * a + b) * 128 : (2 * a + b + 1) * 128, :] += gram(a, b, 1)
    for a, b in rest:
        packed = fold(a, b, packed)
    packed_traces = fold_traces(1, packed_traces)
    own[:, :, 0:128] = packed.reshape(8, 8, 128)
    own[:, :, 128:256] = packed_traces.reshape(8, 8, 128)

    copies = []
    for i in range(1, 8):
        to = lax.rem(ring + i, 8)
        copies.append(remote(own.at[to], part_a.at[ring], sb.at[i], rb.at[i], (to * RING + z, m)))
    for copy in copies:
        copy.start()
    part_a[ring] = own[ring]
    for copy in copies:
        copy.wait()
    part_b[z] = jnp.sum(part_a[...], axis=0)

    copies = []
    for i in range(1, 8):
        to = lax.rem(z + i, 8)
        copies.append(remote(part_b.at[z], part_b.at[z], sc.at[i], rc.at[i], (ring * RING + to, m)))
    for copy in copies:
        copy.start()
    for copy in copies:
        copy.wait()
    part_c[m] = jnp.sum(part_b[...], axis=0)

    copies = []
    for i in range(1, 4):
        to = lax.rem(m + i, 4)
        copies.append(remote(part_c.at[m], part_c.at[m], sd.at[i], rd.at[i], (t, to)))
    for copy in copies:
        copy.start()
    for copy in copies:
        copy.wait()
    last[...] = part_c[0] + part_c[1] + part_c[2] + part_c[3]

    row = jnp.broadcast_to(last[pl.ds(z, 1), :], (8, 256))

    def chosen(index):
        return jnp.dot(
            row, picks[index], preferred_element_type=jnp.float32, precision=lax.Precision.HIGHEST
        )

    here, there = (chosen(1), chosen(2)), (chosen(3), chosen(4))
    box_real = here[0] * there[0] + here[1] * there[1]
    box_imag = here[1] * there[0] - here[0] * there[1]
    box = jnp.where(lanes_of((8, 128), 1) < 24, box_real, box_imag)
    out_ref[...] = jnp.where(lanes_of((8, 128), 0) == 0, chosen(0), box) * (1.0 / N)

    def finish(step, _):
        shifted(step, 0).wait_send()
        for copy in (over_chips, over_cores, over_cores_late):
            copy(step).wait_send()
        return 0

    lax.fori_loop(0, STEPS, finish, 0)
    if ahead != 0:
        left_move.wait_send()


def fused(offset, ahead, delta, pair, left, right):
    vmem = pl.BlockSpec(memory_space=pltpu.VMEM)
    smem = pl.BlockSpec(memory_space=pltpu.SMEM)
    whole = pl.BlockSpec(memory_space=pl.ANY)
    half_float, single = jnp.bfloat16, jnp.float32
    return pl.pallas_call(
        functools.partial(fused_kernel, offset, ahead),
        out_shape=jax.ShapeDtypeStruct((8, 128), single),
        in_specs=[smem, smem, whole, whole],
        out_specs=vmem,
        scratch_shapes=[
            pltpu.VMEM((2, 2, ROWS, N), half_float),
            pltpu.VMEM((2, 2, ROWS, N), half_float),
            pltpu.VMEM((2, 2, ROWS, N), half_float),
            pltpu.VMEM((2, ROWS, N), half_float),
            pltpu.VMEM((STEPS, 2, ROWS, WIDE), half_float),
            pltpu.VMEM((STEPS, 2, N, WIDE), half_float),
            pltpu.VMEM((2, 2, T, 16, WIDE), half_float),
            pltpu.VMEM((2, 2, T, 16, WIDE), half_float),
            pltpu.VMEM((2 * T * 16, 128), single),
            pltpu.VMEM((2, 2, 8, 128, WIDE), half_float),
            pltpu.VMEM((4 * 128, 128), single),
            pltpu.VMEM((5, 256, 128), single),
            pltpu.VMEM((8, 8, 256), single),
            pltpu.VMEM((8, 8, 256), single),
            pltpu.VMEM((8, 8, 256), single),
            pltpu.VMEM((4, 8, 256), single),
            pltpu.VMEM((8, 256), single),
            DMA((2,)), DMA, DMA,
        ]
        + [DMA((STEPS,))] * 8
        + [DMA((2, 2))] * 2
        + [DMA((8,))] * 4
        + [DMA((4,))] * 2,
        compiler_params=pltpu.CompilerParams(
            collective_id=offset, has_side_effects=True, vmem_limit_bytes=48 * MIB
        ),
    )(delta, pair, left, right)


AHEAD = {1: 0, 2: 0, 3: 1, 4: 0, 5: -2, 6: -1}


def on_device(fields_left, fields_right, delta, pair):
    left, right = fields_left[:, :, 0], fields_right[:, :, 0]
    branches = [functools.partial(fused, offset, AHEAD[offset]) for offset in range(1, DMAX)]
    sums = lax.switch(delta[0] + delta[1] - DMAX - 1, branches, delta, pair, left, right)
    shape = (1, 2, 2, 2, 2 * HALF)
    return sums[0, :48].reshape(shape), sums[1, :48].reshape(shape)


def solution(mesh):
    split = P(None, None, "tm", "mode", None)
    out = P("tm", None, None, None, None)
    return jax.shard_map(
        on_device, mesh=mesh, in_specs=(split, split, P(), P()), out_specs=(out, out), check_vma=False
    )
```

```python
import functools

import jax
import jax.numpy as jnp
from jax import lax
from jax.experimental import pallas as pl
from jax.experimental.pallas import tpu as pltpu
from jax.sharding import PartitionSpec as P

HALF = 3
DMAX = 7
MESH = pl.DeviceIdType.MESH
DMA = pltpu.SemaphoreType.DMA
T = 64
RING = 8
ROWS = 256
N = 1024
CHUNKS = 4
WIDE = N // CHUNKS
STEPS = 2 * CHUNKS
MIB = 2**20


def remote(src, dst, send, recv, device):
    return pltpu.make_async_remote_copy(
        src_ref=src, dst_ref=dst, send_sem=send, recv_sem=recv, device_id=device, device_id_type=MESH
    )


def rolled_rows(value):
    row = lax.broadcasted_iota(jnp.int32, value.shape, 0)
    for bit in range(6):
        use = lax.rem(row // (1 << bit), 2) == 1
        value = jnp.where(use, pltpu.roll(value, 128 - (2 << bit), 1), value)
    return value


def lanes_of(shape, axis):
    return lax.broadcasted_iota(jnp.int32, shape, axis)


def fused_kernel(
    offset, ahead, delta_ref, pair_ref, left_ref, right_ref, out_ref,
    left_in, right_in, left_op, left_sent, sent, whole, made, got, wide, folded, grams, picks,
    own, part_a, part_b, part_c, last,
    in_sem, sl, rl, s1, r1, s2, r2, s3, r3, s4, r4, sa, ra, sb, rb, sc, rc,
):
    t, m = lax.axis_index("tm"), lax.axis_index("mode")
    z, ring = lax.rem(t, RING), t // RING
    moves = (DMAX, (offset - ahead) % T)
    loads = [
        pltpu.make_async_copy(right_ref, right_in, in_sem.at[0]),
        pltpu.make_async_copy(left_ref, left_in, in_sem.at[1]),
    ]
    for load in loads:
        load.start()

    across = (t, lax.rem(m + 2, 4))
    core = (t, m + 1 - 2 * lax.rem(m, 2))
    targets, sources = [], []
    for shift in moves:
        later, earlier = lax.rem(t + shift, T), lax.rem(t + T - shift, T)
        flip_in = lax.rem(t // RING + later // RING, 2)
        flip_out = lax.rem(t // RING + earlier // RING, 2)
        sources.append((later, lax.rem(m + 2 * flip_in, 4)))
        targets.append((earlier, lax.rem(m + 2 * flip_out, 4)))

    barrier = pltpu.get_barrier_semaphore()

    def hello(i, _):
        pl.semaphore_signal(barrier, inc=1, device_id=(lax.rem(t + i, T), m), device_id_type=MESH)
        return 0

    for source in sources:
        pl.semaphore_signal(barrier, inc=1, device_id=source, device_id_type=MESH)
    for i in range(1, 4):
        pl.semaphore_signal(barrier, inc=1, device_id=(t, lax.rem(m + i, 4)), device_id_type=MESH)
    lax.fori_loop(1, T, hello, 0)
    for i in range(1, 8):
        other_ring = lax.rem(ring + i, 8) * RING + z
        other_place = ring * RING + lax.rem(z + i, 8)
        for device in ((other_ring, core[1]), (other_place, across[1])):
            pl.semaphore_signal(barrier, inc=1, device_id=device, device_id_type=MESH)

    in_order = delta_ref[0] == DMAX
    first = jnp.where(in_order, pair_ref[0], pair_ref[1])

    loads[0].wait()
    for product in range(2):
        field = first if product == 0 else 1 - first
        for column in range(CHUNKS):
            sent[product * CHUNKS + column] = right_in[field, :, :, column * WIDE : (column + 1) * WIDE]
    pl.semaphore_wait(barrier, T - 1 + 3 + 2 + 14)

    source_modes = (sources[0][1], sources[1][1])

    def block(step, mode):
        return whole.at[step, :, pl.ds(pl.multiple_of(mode * ROWS, ROWS), ROWS), :]

    def shifted(step, product):
        return remote(sent.at[step], block(step, m), s1.at[step], r1.at[step], targets[product])

    def source_mode(step):
        product = step // CHUNKS
        return source_modes[0] * (1 - product) + source_modes[1] * product

    def over_chips(step):
        part = block(step, source_mode(step))
        return remote(part, part, s2.at[step], r2.at[step], across)

    def over_cores(step):
        part = block(step, source_mode(step))
        return remote(part, part, s3.at[step], r3.at[step], core)

    def over_cores_late(step):
        part = block(step, lax.rem(source_mode(step) + 2, 4))
        return remote(part, part, s4.at[step], r4.at[step], core)

    for column in range(2):
        for product in range(2):
            shifted(product * CHUNKS + column, product).start()

    loads[1].wait()
    left_op[0] = left_in[first]
    if ahead == 0:
        left_op[1] = left_in[1 - first]
    else:
        left_sent[...] = left_in[1 - first]
        left_move = remote(left_sent, left_op.at[1], sl, rl, (lax.rem(t + ahead + T, T), m))
        if ahead < 0:
            left_move.start()

    def multiply(step):
        product, column = step // CHUNKS, lax.rem(step, CHUNKS)
        over_cores(step).wait_recv()
        over_cores_late(step).wait_recv()
        real_left, imag_left = left_op[product, 0], left_op[product, 1]
        real_right, imag_right = whole[step, 0], whole[step, 1]
        dot = functools.partial(jnp.dot, preferred_element_type=jnp.float32)
        real = dot(real_left, real_right) - dot(imag_left, imag_right)
        imag = dot(real_left, imag_right) + dot(imag_left, real_right)
        pieces = jnp.concatenate(
            [real.reshape(ROWS // 8, 8, WIDE), imag.reshape(ROWS // 8, 8, WIDE)], axis=1
        ).astype(jnp.bfloat16)
        place = pl.ds(pl.multiple_of(lax.rem(column, 2) * 32, 32), 32)
        made[product, column // 2, place] = pieces

    def spread(product, half):
        slot = lax.rem(t + T - ahead * product, T)

        def send(i, _):
            odd = lax.rem(i, 2)
            far = odd * ((i + 1) // 2) + (1 - odd) * (T - i // 2)
            to = lax.rem(t + far, T)
            remote(
                made.at[product, half, to], got.at[product, half, slot],
                sa.at[product, half], ra.at[product, half], (to, m),
            ).start()
            return 0

        lax.fori_loop(1, T, send, 0)
        got[product, half, slot] = made[product, half, t]

    def turn_of(i, _):
        @pl.when(i < STEPS)
        def _():
            shifted(i, 0).wait_recv()
            over_chips(i).start()
            over_cores(i).start()

        @pl.when(i < 2)
        def _():
            shifted(i + 2, 0).start()

        @pl.when((i >= 2) & (i < 4))
        def _():
            shifted(i + 4, 1).start()

        if ahead > 0:
            @pl.when(i == 2)
            def _():
                left_move.start()

        @pl.when((i >= 1) & (i < STEPS + 1))
        def _():
            over_chips(i - 1).wait_recv()
            over_cores_late(i - 1).start()

        @pl.when((i >= 1) & (i != CHUNKS + 1))
        def _():
            step = i - 1 - i // (CHUNKS + 2)
            if ahead != 0:
                @pl.when(step == CHUNKS)
                def _():
                    left_move.wait_recv()
            multiply(step)

            @pl.when(lax.rem(step, 2) == 1)
            def _():
                spread(step // CHUNKS, lax.rem(step, CHUNKS) // 2)

        return 0

    lax.fori_loop(0, STEPS + 2, turn_of, 0)

    sum_row, lane = lanes_of((256, 128), 0), lanes_of((256, 128), 1)
    part, k, l, s = lane // 24, lax.rem(lane // 12, 2), lax.rem(lane // 6, 2), lax.rem(lane, 6) + 1
    swap = jnp.where(in_order, 0, 1)
    k, l = k + swap - 2 * swap * k, l + swap - 2 * swap * l
    valid = lane < 48

    def pick(index, *terms):
        value = jnp.zeros((256, 128), jnp.float32)
        for where, sign in terms:
            value = value + jnp.where((sum_row == where) & valid, sign, 0.0)
        picks[index] = value

    pair_at = (2 * k + l) * 16 + 2 * s
    sign = jnp.where(part == 0, 1.0, -1.0)
    pick(0, (pair_at + 64 * part, 1.0), (pair_at + 1 + 64 * (1 - part), sign))
    for d in range(2):
        pick(1 + d, (128 + k * 16 + d, 1.0))
        pick(3 + d, (128 + l * 16 + 2 * s + d, 1.0))

    over_lanes = (((1,), (1,)), ((), ()))

    def dot_t(a, b):
        return lax.dot_general(a, b, over_lanes, preferred_element_type=jnp.float32)

    mask_lane = lanes_of((16, WIDE), 1)
    traces = [jnp.zeros((16, 128), jnp.float32) for _ in range(2)]

    def absorb(product, half):
        remote(
            made.at[product, half, pl.ds(0, T - 1)], got.at[product, half, pl.ds(0, T - 1)],
            sa.at[product, half], ra.at[product, half], across,
        ).wait()
        count = T * 16
        for j in range(2):
            piece = got[product, half, :, :, j * 128 : (j + 1) * 128].astype(jnp.float32)
            wide[pl.ds(j * count, count), :] = piece.reshape(count, 128)
        for r in range(8):
            pieces = [wide[pl.ds(j * count + r, 128, stride=8), :] for j in range(2)]
            value = jnp.concatenate(pieces, axis=1).astype(jnp.bfloat16)
            folded[product, half, r] = value
            at = (2 * half + t // 32) * WIDE
            hit = mask_lane + at == m * ROWS + lax.rem(t, 32) * 8 + r
            diagonal = jnp.where(hit, 1.0, 0.0).astype(jnp.bfloat16)
            traces[product] += dot_t(diagonal, value)

    def gram(a, b, half):
        value = jnp.zeros((128, 128), jnp.float32)
        for r in range(8):
            value += dot_t(folded[a, half, r], folded[b, half, r])
        return value

    place = lanes_of((T, 128), 1) // 16

    def fold(a, b, packed):
        for c in range(2):
            index = c * 4 + a * 2 + b
            value = rolled_rows(grams[pl.ds((2 * a + b) * 128 + c, T, stride=2), :])
            value = pltpu.roll(value, 16 * index, 1) if index else value
            packed = jnp.where(place == index, value, packed)
        return packed

    def fold_traces(a, packed):
        value = rolled_rows(jnp.broadcast_to(traces[a][0:1], (T, 128)))
        value = pltpu.roll(value, 16 * a, 1) if a else value
        return jnp.where(place == a, value, packed)

    packed = jnp.zeros((T, 128), jnp.float32)
    packed_traces = jnp.zeros((T, 128), jnp.float32)
    absorb(0, 0)
    grams[0:128, :] = gram(0, 0, 0)
    absorb(0, 1)
    grams[0:128, :] += gram(0, 0, 1)
    packed = fold(0, 0, packed)
    packed_traces = fold_traces(0, packed_traces)
    rest = ((0, 1), (1, 0), (1, 1))
    absorb(1, 0)
    for a, b in rest:
        grams[(2 * a + b) * 128 : (2 * a + b + 1) * 128, :] = gram(a, b, 0)
    absorb(1, 1)
    for a, b in rest:
        grams[(2 * a + b) * 128 : (2 * a + b + 1) * 128, :] += gram(a, b, 1)
    for a, b in rest:
        packed = fold(a, b, packed)
    packed_traces = fold_traces(1, packed_traces)
    own[:, :, 0:128] = packed.reshape(8, 8, 128)
    own[:, :, 128:256] = packed_traces.reshape(8, 8, 128)

    def everyone(buffer, mine, source_of, send, recv, to):
        copies = []
        for i in range(1, 16):
            target, device = to(i)
            copies.append(remote(source_of(target), buffer.at[mine], send.at[i], recv.at[i], device))
            copies[-1].start()
        buffer[mine] = source_of(mine)[...]
        for copy in copies:
            copy.wait_recv()
        total = buffer[0]
        for i in range(1, 16):
            total = total + buffer[i]
        return total, copies

    def over_rings(i):
        to = lax.rem(mine_a + i, 16)
        return to, ((to // 2) * RING + z, m // 2 * 2 + lax.rem(to, 2))

    def over_places(i):
        to = lax.rem(mine_b + i, 16)
        return to, (ring * RING + to // 2, lax.rem(to, 2) * 2 + lax.rem(m, 2))

    mine_a, mine_b = ring * 2 + lax.rem(m, 2), z * 2 + m // 2
    total, sent_a = everyone(part_a, mine_a, lambda target: own.at[target // 2], sb, rb, over_rings)
    part_c[...] = total
    total, sent_b = everyone(part_b, mine_b, lambda target: part_c, sc, rc, over_places)
    last[...] = total

    row = jnp.broadcast_to(last[pl.ds(z, 1), :], (8, 256))

    def chosen(index):
        return jnp.dot(
            row, picks[index], preferred_element_type=jnp.float32, precision=lax.Precision.HIGHEST
        )

    here, there = (chosen(1), chosen(2)), (chosen(3), chosen(4))
    box_real = here[0] * there[0] + here[1] * there[1]
    box_imag = here[1] * there[0] - here[0] * there[1]
    box = jnp.where(lanes_of((8, 128), 1) < 24, box_real, box_imag)
    out_ref[...] = jnp.where(lanes_of((8, 128), 0) == 0, chosen(0), box) * (1.0 / N)

    def finish(step, _):
        shifted(step, 0).wait_send()
        for copy in (over_chips, over_cores, over_cores_late):
            copy(step).wait_send()
        return 0

    lax.fori_loop(0, STEPS, finish, 0)
    for copy in sent_a + sent_b:
        copy.wait_send()
    if ahead != 0:
        left_move.wait_send()


def fused(offset, ahead, delta, pair, left, right):
    vmem = pl.BlockSpec(memory_space=pltpu.VMEM)
    smem = pl.BlockSpec(memory_space=pltpu.SMEM)
    whole = pl.BlockSpec(memory_space=pl.ANY)
    half_float, single = jnp.bfloat16, jnp.float32
    return pl.pallas_call(
        functools.partial(fused_kernel, offset, ahead),
        out_shape=jax.ShapeDtypeStruct((8, 128), single),
        in_specs=[smem, smem, whole, whole],
        out_specs=vmem,
        scratch_shapes=[
            pltpu.VMEM((2, 2, ROWS, N), half_float),
            pltpu.VMEM((2, 2, ROWS, N), half_float),
            pltpu.VMEM((2, 2, ROWS, N), half_float),
            pltpu.VMEM((2, ROWS, N), half_float),
            pltpu.VMEM((STEPS, 2, ROWS, WIDE), half_float),
            pltpu.VMEM((STEPS, 2, N, WIDE), half_float),
            pltpu.VMEM((2, 2, T, 16, WIDE), half_float),
            pltpu.VMEM((2, 2, T, 16, WIDE), half_float),
            pltpu.VMEM((2 * T * 16, 128), single),
            pltpu.VMEM((2, 2, 8, 128, WIDE), half_float),
            pltpu.VMEM((4 * 128, 128), single),
            pltpu.VMEM((5, 256, 128), single),
            pltpu.VMEM((8, 8, 256), single),
            pltpu.VMEM((16, 8, 256), single),
            pltpu.VMEM((16, 8, 256), single),
            pltpu.VMEM((8, 256), single),
            pltpu.VMEM((8, 256), single),
            DMA((2,)), DMA, DMA,
        ]
        + [DMA((STEPS,))] * 8
        + [DMA((2, 2))] * 2
        + [DMA((16,))] * 4,
        compiler_params=pltpu.CompilerParams(
            collective_id=offset, has_side_effects=True, vmem_limit_bytes=48 * MIB
        ),
    )(delta, pair, left, right)


AHEAD = {1: 0, 2: 0, 3: 1, 4: 0, 5: -2, 6: -1}


def on_device(fields_left, fields_right, delta, pair):
    left, right = fields_left[:, :, 0], fields_right[:, :, 0]
    branches = [functools.partial(fused, offset, AHEAD[offset]) for offset in range(1, DMAX)]
    sums = lax.switch(delta[0] + delta[1] - DMAX - 1, branches, delta, pair, left, right)
    shape = (1, 2, 2, 2, 2 * HALF)
    return sums[0, :48].reshape(shape), sums[1, :48].reshape(shape)


def solution(mesh):
    split = P(None, None, "tm", "mode", None)
    out = P("tm", None, None, None, None)
    return jax.shard_map(
        on_device, mesh=mesh, in_specs=(split, split, P(), P()), out_specs=(out, out), check_vma=False
    )
```

```python
import functools

import jax
import jax.numpy as jnp
from jax import lax
from jax.experimental import pallas as pl
from jax.experimental.pallas import tpu as pltpu
from jax.sharding import PartitionSpec as P

HALF = 3
DMAX = 7
MESH = pl.DeviceIdType.MESH
DMA = pltpu.SemaphoreType.DMA
T = 64
RING = 8
ROWS = 256
N = 1024
CHUNKS = 4
WIDE = N // CHUNKS
STEPS = 2 * CHUNKS
MIB = 2**20


def remote(src, dst, send, recv, device):
    return pltpu.make_async_remote_copy(
        src_ref=src, dst_ref=dst, send_sem=send, recv_sem=recv, device_id=device, device_id_type=MESH
    )


def rolled_rows(value):
    row = lax.broadcasted_iota(jnp.int32, value.shape, 0)
    for bit in range(6):
        use = lax.rem(row // (1 << bit), 2) == 1
        value = jnp.where(use, pltpu.roll(value, 128 - (2 << bit), 1), value)
    return value


def lanes_of(shape, axis):
    return lax.broadcasted_iota(jnp.int32, shape, axis)


def fused_kernel(
    offset, ahead, delta_ref, pair_ref, left_ref, right_ref, out_ref,
    left_in, right_in, left_op, left_sent, sent, whole, made, got, wide, folded, grams, picks,
    own, part_a, part_b, part_c, last,
    in_sem, sl, rl, s1, r1, s2, r2, s3, r3, s4, r4, sa, ra, sb, rb, sc, rc,
):
    t, m = lax.axis_index("tm"), lax.axis_index("mode")
    z, ring = lax.rem(t, RING), t // RING
    moves = (DMAX, (offset - ahead) % T)
    loads = [
        pltpu.make_async_copy(right_ref, right_in, in_sem.at[0]),
        pltpu.make_async_copy(left_ref, left_in, in_sem.at[1]),
    ]
    for load in loads:
        load.start()

    across = (t, lax.rem(m + 2, 4))
    core = (t, m + 1 - 2 * lax.rem(m, 2))
    targets, sources = [], []
    for shift in moves:
        later, earlier = lax.rem(t + shift, T), lax.rem(t + T - shift, T)
        flip_in = lax.rem(t // RING + later // RING, 2)
        flip_out = lax.rem(t // RING + earlier // RING, 2)
        sources.append((later, lax.rem(m + 2 * flip_in, 4)))
        targets.append((earlier, lax.rem(m + 2 * flip_out, 4)))

    barrier = pltpu.get_barrier_semaphore()

    def hello(to, _):
        pl.semaphore_signal(barrier, inc=1, device_id=(to, m), device_id_type=MESH)
        return 0

    for source in sources:
        pl.semaphore_signal(barrier, inc=1, device_id=source, device_id_type=MESH)
    for i in range(1, 4):
        pl.semaphore_signal(barrier, inc=1, device_id=(t, lax.rem(m + i, 4)), device_id_type=MESH)
    lax.fori_loop(t + 1, T, hello, 0)
    lax.fori_loop(0, t, hello, 0)
    for i in range(1, 8):
        other_ring = lax.rem(ring + i, 8) * RING + z
        other_place = ring * RING + lax.rem(z + i, 8)
        for device in ((other_ring, core[1]), (other_place, across[1])):
            pl.semaphore_signal(barrier, inc=1, device_id=device, device_id_type=MESH)

    in_order = delta_ref[0] == DMAX
    first = jnp.where(in_order, pair_ref[0], pair_ref[1])

    loads[0].wait()
    for product in range(2):
        field = first if product == 0 else 1 - first
        for column in range(CHUNKS):
            sent[product * CHUNKS + column] = right_in[field, :, :, column * WIDE : (column + 1) * WIDE]
    pl.semaphore_wait(barrier, T - 1 + 3 + 2 + 14)

    source_modes = (sources[0][1], sources[1][1])

    def block(step, mode):
        return whole.at[step, :, pl.ds(pl.multiple_of(mode * ROWS, ROWS), ROWS), :]

    def shifted(step, product):
        return remote(sent.at[step], block(step, m), s1.at[step], r1.at[step], targets[product])

    def source_mode(step):
        product = step // CHUNKS
        return source_modes[0] * (1 - product) + source_modes[1] * product

    def over_chips(step):
        part = block(step, source_mode(step))
        return remote(part, part, s2.at[step], r2.at[step], across)

    def over_cores(step):
        part = block(step, source_mode(step))
        return remote(part, part, s3.at[step], r3.at[step], core)

    def over_cores_late(step):
        part = block(step, lax.rem(source_mode(step) + 2, 4))
        return remote(part, part, s4.at[step], r4.at[step], core)

    wait_for_first = offset in FIRST_ALONE
    for column in range(2):
        shifted(column, 0).start()
        if not wait_for_first:
            shifted(CHUNKS + column, 1).start()

    loads[1].wait()
    left_op[0] = left_in[first]
    if ahead == 0:
        left_op[1] = left_in[1 - first]
    else:
        left_sent[...] = left_in[1 - first]
        left_move = remote(left_sent, left_op.at[1], sl, rl, (lax.rem(t + ahead + T, T), m))
        if ahead < 0:
            left_move.start()

    def multiply(step):
        product, column = step // CHUNKS, lax.rem(step, CHUNKS)
        over_cores(step).wait_recv()
        over_cores_late(step).wait_recv()
        real_left, imag_left = left_op[product, 0], left_op[product, 1]
        real_right, imag_right = whole[step, 0], whole[step, 1]
        dot = functools.partial(jnp.dot, preferred_element_type=jnp.float32)
        real = dot(real_left, real_right) - dot(imag_left, imag_right)
        imag = dot(real_left, imag_right) + dot(imag_left, real_right)
        pieces = jnp.concatenate(
            [real.reshape(ROWS // 8, 8, WIDE), imag.reshape(ROWS // 8, 8, WIDE)], axis=1
        ).astype(jnp.bfloat16)
        place = pl.ds(pl.multiple_of(lax.rem(column, 2) * 32, 32), 32)
        made[product, column // 2, place] = pieces

    def spread(product, half):
        slot = lax.rem(t + T - ahead * product, T)

        def send(to, _):
            remote(
                made.at[product, half, to], got.at[product, half, slot],
                sa.at[product, half], ra.at[product, half], (to, m),
            ).start()
            return 0

        lax.fori_loop(t + 1, T, send, 0)
        lax.fori_loop(0, t, send, 0)
        got[product, half, slot] = made[product, half, t]

    def turn_of(i, _):
        @pl.when(i < STEPS)
        def _():
            shifted(i, 0).wait_recv()
            over_chips(i).start()
            over_cores(i).start()

        @pl.when(i < 2)
        def _():
            shifted(i + 2, 0).start()
            if wait_for_first:
                shifted(i + CHUNKS, 1).start()

        @pl.when((i >= 2) & (i < 4))
        def _():
            shifted(i + 4, 1).start()

        if ahead > 0:
            @pl.when(i == 2)
            def _():
                left_move.start()

        @pl.when((i >= 1) & (i < STEPS + 1))
        def _():
            over_chips(i - 1).wait_recv()
            over_cores_late(i - 1).start()

        @pl.when((i >= 1) & (i != CHUNKS + 1))
        def _():
            step = i - 1 - i // (CHUNKS + 2)
            if ahead != 0:
                @pl.when(step == CHUNKS)
                def _():
                    left_move.wait_recv()
            multiply(step)

            @pl.when(lax.rem(step, 2) == 1)
            def _():
                spread(step // CHUNKS, lax.rem(step, CHUNKS) // 2)

        return 0

    lax.fori_loop(0, STEPS + 2, turn_of, 0)

    sum_row, lane = lanes_of((256, 128), 0), lanes_of((256, 128), 1)
    part, k, l, s = lane // 24, lax.rem(lane // 12, 2), lax.rem(lane // 6, 2), lax.rem(lane, 6) + 1
    swap = jnp.where(in_order, 0, 1)
    k, l = k + swap - 2 * swap * k, l + swap - 2 * swap * l
    valid = lane < 48

    def pick(index, *terms):
        value = jnp.zeros((256, 128), jnp.float32)
        for where, sign in terms:
            value = value + jnp.where((sum_row == where) & valid, sign, 0.0)
        picks[index] = value

    pair_at = (2 * k + l) * 16 + 2 * s
    sign = jnp.where(part == 0, 1.0, -1.0)
    pick(0, (pair_at + 64 * part, 1.0), (pair_at + 1 + 64 * (1 - part), sign))
    for d in range(2):
        pick(1 + d, (128 + k * 16 + d, 1.0))
        pick(3 + d, (128 + l * 16 + 2 * s + d, 1.0))

    over_lanes = (((1,), (1,)), ((), ()))

    def dot_t(a, b):
        return lax.dot_general(a, b, over_lanes, preferred_element_type=jnp.float32)

    mask_lane = lanes_of((16, WIDE), 1)
    traces = [jnp.zeros((16, 128), jnp.float32) for _ in range(2)]

    def absorb(product, half):
        remote(
            made.at[product, half, pl.ds(0, T - 1)], got.at[product, half, pl.ds(0, T - 1)],
            sa.at[product, half], ra.at[product, half], across,
        ).wait()
        count = T * 16
        for j in range(2):
            piece = got[product, half, :, :, j * 128 : (j + 1) * 128].astype(jnp.float32)
            wide[pl.ds(j * count, count), :] = piece.reshape(count, 128)
        for r in range(8):
            pieces = [wide[pl.ds(j * count + r, 128, stride=8), :] for j in range(2)]
            value = jnp.concatenate(pieces, axis=1).astype(jnp.bfloat16)
            folded[product, half, r] = value
            at = (2 * half + t // 32) * WIDE
            hit = mask_lane + at == m * ROWS + lax.rem(t, 32) * 8 + r
            diagonal = jnp.where(hit, 1.0, 0.0).astype(jnp.bfloat16)
            traces[product] += dot_t(diagonal, value)

    def gram(a, b, half):
        value = jnp.zeros((128, 128), jnp.float32)
        for r in range(8):
            value += dot_t(folded[a, half, r], folded[b, half, r])
        return value

    place = lanes_of((T, 128), 1) // 16

    def fold(a, b, packed):
        for c in range(2):
            index = c * 4 + a * 2 + b
            value = rolled_rows(grams[pl.ds((2 * a + b) * 128 + c, T, stride=2), :])
            value = pltpu.roll(value, 16 * index, 1) if index else value
            packed = jnp.where(place == index, value, packed)
        return packed

    def fold_traces(a, packed):
        value = rolled_rows(jnp.broadcast_to(traces[a][0:1], (T, 128)))
        value = pltpu.roll(value, 16 * a, 1) if a else value
        return jnp.where(place == a, value, packed)

    packed = jnp.zeros((T, 128), jnp.float32)
    packed_traces = jnp.zeros((T, 128), jnp.float32)
    absorb(0, 0)
    grams[0:128, :] = gram(0, 0, 0)
    absorb(0, 1)
    grams[0:128, :] += gram(0, 0, 1)
    packed = fold(0, 0, packed)
    packed_traces = fold_traces(0, packed_traces)
    rest = ((0, 1), (1, 0), (1, 1))
    absorb(1, 0)
    for a, b in rest:
        grams[(2 * a + b) * 128 : (2 * a + b + 1) * 128, :] = gram(a, b, 0)
    absorb(1, 1)
    for a, b in rest:
        grams[(2 * a + b) * 128 : (2 * a + b + 1) * 128, :] += gram(a, b, 1)
    for a, b in rest:
        packed = fold(a, b, packed)
    packed_traces = fold_traces(1, packed_traces)
    own[:, :, 0:128] = packed.reshape(8, 8, 128)
    own[:, :, 128:256] = packed_traces.reshape(8, 8, 128)

    def everyone(buffer, mine, source_of, send, recv, to):
        copies = []
        for i in range(1, 16):
            target, device = to(i)
            copies.append(remote(source_of(target), buffer.at[mine], send.at[i], recv.at[i], device))
            copies[-1].start()
        buffer[mine] = source_of(mine)[...]
        for copy in copies:
            copy.wait_recv()
        total = buffer[0]
        for i in range(1, 16):
            total = total + buffer[i]
        return total, copies

    def over_rings(i):
        to = lax.rem(mine_a + i, 16)
        return to, ((to // 2) * RING + z, m // 2 * 2 + lax.rem(to, 2))

    def over_places(i):
        to = lax.rem(mine_b + i, 16)
        return to, (ring * RING + to // 2, lax.rem(to, 2) * 2 + lax.rem(m, 2))

    mine_a, mine_b = ring * 2 + lax.rem(m, 2), z * 2 + m // 2
    total, sent_a = everyone(part_a, mine_a, lambda target: own.at[target // 2], sb, rb, over_rings)
    part_c[...] = total
    total, sent_b = everyone(part_b, mine_b, lambda target: part_c, sc, rc, over_places)
    last[...] = total

    row = jnp.broadcast_to(last[pl.ds(z, 1), :], (8, 256))

    def chosen(index):
        return jnp.dot(
            row, picks[index], preferred_element_type=jnp.float32, precision=lax.Precision.HIGHEST
        )

    here, there = (chosen(1), chosen(2)), (chosen(3), chosen(4))
    box_real = here[0] * there[0] + here[1] * there[1]
    box_imag = here[1] * there[0] - here[0] * there[1]
    box = jnp.where(lanes_of((8, 128), 1) < 24, box_real, box_imag)
    out_ref[...] = jnp.where(lanes_of((8, 128), 0) == 0, chosen(0), box) * (1.0 / N)

    def finish(step, _):
        shifted(step, 0).wait_send()
        for copy in (over_chips, over_cores, over_cores_late):
            copy(step).wait_send()
        return 0

    lax.fori_loop(0, STEPS, finish, 0)
    for copy in sent_a + sent_b:
        copy.wait_send()
    if ahead != 0:
        left_move.wait_send()


def fused(offset, ahead, delta, pair, left, right):
    vmem = pl.BlockSpec(memory_space=pltpu.VMEM)
    smem = pl.BlockSpec(memory_space=pltpu.SMEM)
    whole = pl.BlockSpec(memory_space=pl.ANY)
    half_float, single = jnp.bfloat16, jnp.float32
    return pl.pallas_call(
        functools.partial(fused_kernel, offset, ahead),
        out_shape=jax.ShapeDtypeStruct((8, 128), single),
        in_specs=[smem, smem, whole, whole],
        out_specs=vmem,
        scratch_shapes=[
            pltpu.VMEM((2, 2, ROWS, N), half_float),
            pltpu.VMEM((2, 2, ROWS, N), half_float),
            pltpu.VMEM((2, 2, ROWS, N), half_float),
            pltpu.VMEM((2, ROWS, N), half_float),
            pltpu.VMEM((STEPS, 2, ROWS, WIDE), half_float),
            pltpu.VMEM((STEPS, 2, N, WIDE), half_float),
            pltpu.VMEM((2, 2, T, 16, WIDE), half_float),
            pltpu.VMEM((2, 2, T, 16, WIDE), half_float),
            pltpu.VMEM((2 * T * 16, 128), single),
            pltpu.VMEM((2, 2, 8, 128, WIDE), half_float),
            pltpu.VMEM((4 * 128, 128), single),
            pltpu.VMEM((5, 256, 128), single),
            pltpu.VMEM((8, 8, 256), single),
            pltpu.VMEM((16, 8, 256), single),
            pltpu.VMEM((16, 8, 256), single),
            pltpu.VMEM((8, 256), single),
            pltpu.VMEM((8, 256), single),
            DMA((2,)), DMA, DMA,
        ]
        + [DMA((STEPS,))] * 8
        + [DMA((2, 2))] * 2
        + [DMA((16,))] * 4,
        compiler_params=pltpu.CompilerParams(
            collective_id=offset, has_side_effects=True, vmem_limit_bytes=48 * MIB
        ),
    )(delta, pair, left, right)


AHEAD = {1: 0, 2: 0, 3: 1, 4: 0, 5: -2, 6: -1}
FIRST_ALONE = (1, 2, 3, 5, 6)


def on_device(fields_left, fields_right, delta, pair):
    left, right = fields_left[:, :, 0], fields_right[:, :, 0]
    branches = [functools.partial(fused, offset, AHEAD[offset]) for offset in range(1, DMAX)]
    sums = lax.switch(delta[0] + delta[1] - DMAX - 1, branches, delta, pair, left, right)
    shape = (1, 2, 2, 2, 2 * HALF)
    return sums[0, :48].reshape(shape), sums[1, :48].reshape(shape)


def solution(mesh):
    split = P(None, None, "tm", "mode", None)
    out = P("tm", None, None, None, None)
    return jax.shard_map(
        on_device, mesh=mesh, in_specs=(split, split, P(), P()), out_specs=(out, out), check_vma=False
    )
```

```python
import functools

import jax
import jax.numpy as jnp
from jax import lax
from jax.experimental import pallas as pl
from jax.experimental.pallas import tpu as pltpu
from jax.sharding import PartitionSpec as P

HALF = 3
DMAX = 7
MESH = pl.DeviceIdType.MESH
DMA = pltpu.SemaphoreType.DMA
T = 64
RING = 8
ROWS = 256
N = 1024
CHUNKS = 4
WIDE = N // CHUNKS
STEPS = 2 * CHUNKS
MIB = 2**20


def remote(src, dst, send, recv, device):
    return pltpu.make_async_remote_copy(
        src_ref=src, dst_ref=dst, send_sem=send, recv_sem=recv, device_id=device, device_id_type=MESH
    )


def rolled_rows(value):
    row = lax.broadcasted_iota(jnp.int32, value.shape, 0)
    for bit in range(6):
        use = lax.rem(row // (1 << bit), 2) == 1
        value = jnp.where(use, pltpu.roll(value, 128 - (2 << bit), 1), value)
    return value


def lanes_of(shape, axis):
    return lax.broadcasted_iota(jnp.int32, shape, axis)


def fused_kernel(
    offset, ahead, delta_ref, pair_ref, left_ref, right_ref, out_ref,
    left_in, right_in, left_op, left_sent, sent, whole, made, got, wide, folded, grams, picks,
    own, part_a, part_b, part_c, last,
    in_sem, sl, rl, s1, r1, s2, r2, s3, r3, s4, r4, sa, ra, sb, rb, sc, rc,
):
    t, m = lax.axis_index("tm"), lax.axis_index("mode")
    z, ring = lax.rem(t, RING), t // RING
    moves = (DMAX, (offset - ahead) % T)
    loads = [
        pltpu.make_async_copy(right_ref, right_in, in_sem.at[0]),
        pltpu.make_async_copy(left_ref, left_in, in_sem.at[1]),
    ]
    for load in loads:
        load.start()

    across = (t, lax.rem(m + 2, 4))
    core = (t, m + 1 - 2 * lax.rem(m, 2))
    targets, sources = [], []
    for shift in moves:
        later, earlier = lax.rem(t + shift, T), lax.rem(t + T - shift, T)
        flip_in = lax.rem(t // RING + later // RING, 2)
        flip_out = lax.rem(t // RING + earlier // RING, 2)
        sources.append((later, lax.rem(m + 2 * flip_in, 4)))
        targets.append((earlier, lax.rem(m + 2 * flip_out, 4)))

    barrier = pltpu.get_barrier_semaphore()

    def hello(to, _):
        pl.semaphore_signal(barrier, inc=1, device_id=(to, m), device_id_type=MESH)
        return 0

    for source in sources:
        pl.semaphore_signal(barrier, inc=1, device_id=source, device_id_type=MESH)
    for i in range(1, 4):
        pl.semaphore_signal(barrier, inc=1, device_id=(t, lax.rem(m + i, 4)), device_id_type=MESH)
    lax.fori_loop(t + 1, T, hello, 0)
    lax.fori_loop(0, t, hello, 0)
    for i in range(1, 8):
        other_ring = lax.rem(ring + i, 8) * RING + z
        other_place = ring * RING + lax.rem(z + i, 8)
        for device in ((other_ring, core[1]), (other_place, across[1])):
            pl.semaphore_signal(barrier, inc=1, device_id=device, device_id_type=MESH)

    in_order = delta_ref[0] == DMAX
    first = jnp.where(in_order, pair_ref[0], pair_ref[1])

    loads[0].wait()
    for product in range(2):
        field = first if product == 0 else 1 - first
        for column in range(CHUNKS):
            sent[product * CHUNKS + column] = right_in[field, :, :, column * WIDE : (column + 1) * WIDE]
    pl.semaphore_wait(barrier, T - 1 + 3 + 2 + 14)

    source_modes = (sources[0][1], sources[1][1])

    def block(step, mode):
        return whole.at[step, :, pl.ds(pl.multiple_of(mode * ROWS, ROWS), ROWS), :]

    def shifted(step, product):
        return remote(sent.at[step], block(step, m), s1.at[step], r1.at[step], targets[product])

    def source_mode(step):
        product = step // CHUNKS
        return source_modes[0] * (1 - product) + source_modes[1] * product

    def over_chips(step):
        part = block(step, source_mode(step))
        return remote(part, part, s2.at[step], r2.at[step], across)

    def over_cores(step):
        part = block(step, source_mode(step))
        return remote(part, part, s3.at[step], r3.at[step], core)

    def over_cores_late(step):
        part = block(step, lax.rem(source_mode(step) + 2, 4))
        return remote(part, part, s4.at[step], r4.at[step], core)

    wait_for_first = offset in FIRST_ALONE
    for column in range(2):
        shifted(column, 0).start()
        if not wait_for_first:
            shifted(CHUNKS + column, 1).start()

    loads[1].wait()
    left_op[0] = left_in[first]
    if ahead == 0:
        left_op[1] = left_in[1 - first]
    else:
        left_sent[...] = left_in[1 - first]
        left_move = remote(left_sent, left_op.at[1], sl, rl, (lax.rem(t + ahead + T, T), m))
        if ahead < 0:
            left_move.start()

    def multiply(step):
        product, column = step // CHUNKS, lax.rem(step, CHUNKS)
        over_cores(step).wait_recv()
        over_cores_late(step).wait_recv()
        real_left, imag_left = left_op[product, 0], left_op[product, 1]
        real_right, imag_right = whole[step, 0], whole[step, 1]
        dot = functools.partial(jnp.dot, preferred_element_type=jnp.float32)
        real = dot(real_left, real_right) - dot(imag_left, imag_right)
        imag = dot(real_left, imag_right) + dot(imag_left, real_right)
        pieces = jnp.concatenate(
            [real.reshape(ROWS // 8, 8, WIDE), imag.reshape(ROWS // 8, 8, WIDE)], axis=1
        ).astype(jnp.bfloat16)
        place = pl.ds(pl.multiple_of(lax.rem(column, 2) * 32, 32), 32)
        made[product, column // 2, place] = pieces

    def spread(product, half):
        slot = lax.rem(t + T - ahead * product, T)

        def send(to, _):
            remote(
                made.at[product, half, to], got.at[product, half, slot],
                sa.at[product, half], ra.at[product, half], (to, m),
            ).start()
            return 0

        lax.fori_loop(t + 1, T, send, 0)
        lax.fori_loop(0, t, send, 0)
        got[product, half, slot] = made[product, half, t]

    def turn_of(i, _):
        @pl.when(i < STEPS)
        def _():
            shifted(i, 0).wait_recv()
            over_chips(i).start()
            over_cores(i).start()

        @pl.when(i < 2)
        def _():
            shifted(i + 2, 0).start()
            if wait_for_first:
                shifted(i + CHUNKS, 1).start()

        @pl.when((i >= 2) & (i < 4))
        def _():
            shifted(i + 4, 1).start()

        if ahead > 0:
            @pl.when(i == 2)
            def _():
                left_move.start()

        @pl.when((i >= 1) & (i < STEPS + 1))
        def _():
            over_chips(i - 1).wait_recv()
            over_cores_late(i - 1).start()

        @pl.when((i >= 1) & (i != CHUNKS + 1))
        def _():
            step = i - 1 - i // (CHUNKS + 2)
            if ahead != 0:
                @pl.when(step == CHUNKS)
                def _():
                    left_move.wait_recv()
            multiply(step)

            @pl.when(lax.rem(step, 2) == 1)
            def _():
                spread(step // CHUNKS, lax.rem(step, CHUNKS) // 2)

        return 0

    lax.fori_loop(0, STEPS + 2, turn_of, 0)

    sum_row, lane = lanes_of((256, 128), 0), lanes_of((256, 128), 1)
    part, k, l, s = lane // 24, lax.rem(lane // 12, 2), lax.rem(lane // 6, 2), lax.rem(lane, 6) + 1
    swap = jnp.where(in_order, 0, 1)
    k, l = k + swap - 2 * swap * k, l + swap - 2 * swap * l
    valid = lane < 48

    def pick(index, *terms):
        value = jnp.zeros((256, 128), jnp.float32)
        for where, sign in terms:
            value = value + jnp.where((sum_row == where) & valid, sign, 0.0)
        picks[index] = value

    pair_at = (2 * k + l) * 16 + 2 * s
    sign = jnp.where(part == 0, 1.0, -1.0)
    pick(0, (pair_at + 64 * part, 1.0), (pair_at + 1 + 64 * (1 - part), sign))
    for d in range(2):
        pick(1 + d, (128 + k * 16 + d, 1.0))
        pick(3 + d, (128 + l * 16 + 2 * s + d, 1.0))

    over_lanes = (((1,), (1,)), ((), ()))

    def dot_t(a, b):
        return lax.dot_general(a, b, over_lanes, preferred_element_type=jnp.float32)

    mask_lane = lanes_of((16, WIDE), 1)
    traces = [jnp.zeros((16, 128), jnp.float32) for _ in range(2)]

    def absorb(product, half):
        remote(
            made.at[product, half, pl.ds(0, T - 1)], got.at[product, half, pl.ds(0, T - 1)],
            sa.at[product, half], ra.at[product, half], across,
        ).wait()
        count = T * 16
        for j in range(2):
            piece = got[product, half, :, :, j * 128 : (j + 1) * 128].astype(jnp.float32)
            wide[pl.ds(j * count, count), :] = piece.reshape(count, 128)
        for r in range(8):
            pieces = [wide[pl.ds(j * count + r, 128, stride=8), :] for j in range(2)]
            value = jnp.concatenate(pieces, axis=1).astype(jnp.bfloat16)
            folded[product, half, r] = value
            at = (2 * half + t // 32) * WIDE
            hit = mask_lane + at == m * ROWS + lax.rem(t, 32) * 8 + r
            diagonal = jnp.where(hit, 1.0, 0.0).astype(jnp.bfloat16)
            traces[product] += dot_t(diagonal, value)

    def gram(a, b, half):
        value = jnp.zeros((128, 128), jnp.float32)
        for r in range(8):
            value += dot_t(folded[a, half, r], folded[b, half, r])
        return value

    place = lanes_of((T, 128), 1) // 16

    def fold(a, b, packed):
        for c in range(2):
            index = c * 4 + a * 2 + b
            value = rolled_rows(grams[pl.ds((2 * a + b) * 128 + c, T, stride=2), :])
            value = pltpu.roll(value, 16 * index, 1) if index else value
            packed = jnp.where(place == index, value, packed)
        return packed

    def fold_traces(a, packed):
        value = rolled_rows(jnp.broadcast_to(traces[a][0:1], (T, 128)))
        value = pltpu.roll(value, 16 * a, 1) if a else value
        return jnp.where(place == a, value, packed)

    packed = jnp.zeros((T, 128), jnp.float32)
    packed_traces = jnp.zeros((T, 128), jnp.float32)
    absorb(0, 0)
    grams[0:128, :] = gram(0, 0, 0)
    absorb(0, 1)
    grams[0:128, :] += gram(0, 0, 1)
    packed = fold(0, 0, packed)
    packed_traces = fold_traces(0, packed_traces)
    rest = ((0, 1), (1, 0), (1, 1))
    absorb(1, 0)
    for a, b in rest:
        grams[(2 * a + b) * 128 : (2 * a + b + 1) * 128, :] = gram(a, b, 0)
    absorb(1, 1)
    for a, b in rest:
        grams[(2 * a + b) * 128 : (2 * a + b + 1) * 128, :] += gram(a, b, 1)
    for a, b in rest:
        packed = fold(a, b, packed)
    packed_traces = fold_traces(1, packed_traces)
    own[:, :, 0:128] = packed.reshape(8, 8, 128)
    own[:, :, 128:256] = packed_traces.reshape(8, 8, 128)

    def everyone(buffer, mine, source_of, send, recv, to):
        copies = []
        for i in range(1, 16):
            target, device = to(i)
            copies.append(remote(source_of(target), buffer.at[mine], send.at[i], recv.at[i], device))
            copies[-1].start()
        buffer[mine] = source_of(mine)[...]
        for copy in copies:
            copy.wait_recv()
        total = buffer[0]
        for i in range(1, 16):
            total = total + buffer[i]
        return total, copies

    def over_rings(i):
        to = lax.rem(mine_a + i, 16)
        return to, ((to // 2) * RING + z, m // 2 * 2 + lax.rem(to, 2))

    def over_places(i):
        to = lax.rem(mine_b + i, 16)
        return to, (ring * RING + to // 2, lax.rem(to, 2) * 2 + lax.rem(m, 2))

    mine_a, mine_b = ring * 2 + lax.rem(m, 2), z * 2 + m // 2
    total, sent_a = everyone(part_a, mine_a, lambda target: own.at[target // 2], sb, rb, over_rings)
    part_c[...] = total
    total, sent_b = everyone(part_b, mine_b, lambda target: part_c, sc, rc, over_places)
    last[...] = total

    row = jnp.broadcast_to(last[pl.ds(z, 1), :], (8, 256))

    def chosen(index):
        return jnp.dot(
            row, picks[index], preferred_element_type=jnp.float32, precision=lax.Precision.HIGHEST
        )

    here, there = (chosen(1), chosen(2)), (chosen(3), chosen(4))
    box_real = here[0] * there[0] + here[1] * there[1]
    box_imag = here[1] * there[0] - here[0] * there[1]
    box = jnp.where(lanes_of((8, 128), 1) < 24, box_real, box_imag)
    out_ref[...] = jnp.where(lanes_of((8, 128), 0) == 0, chosen(0), box) * (1.0 / N)

    def finish(step, _):
        shifted(step, 0).wait_send()
        for copy in (over_chips, over_cores, over_cores_late):
            copy(step).wait_send()
        return 0

    lax.fori_loop(0, STEPS, finish, 0)
    for copy in sent_a + sent_b:
        copy.wait_send()
    if ahead != 0:
        left_move.wait_send()


def fused(offset, ahead, delta, pair, left, right):
    vmem = pl.BlockSpec(memory_space=pltpu.VMEM)
    smem = pl.BlockSpec(memory_space=pltpu.SMEM)
    whole = pl.BlockSpec(memory_space=pl.ANY)
    half_float, single = jnp.bfloat16, jnp.float32
    return pl.pallas_call(
        functools.partial(fused_kernel, offset, ahead),
        out_shape=jax.ShapeDtypeStruct((8, 128), single),
        in_specs=[smem, smem, whole, whole],
        out_specs=vmem,
        scratch_shapes=[
            pltpu.VMEM((2, 2, ROWS, N), half_float),
            pltpu.VMEM((2, 2, ROWS, N), half_float),
            pltpu.VMEM((2, 2, ROWS, N), half_float),
            pltpu.VMEM((2, ROWS, N), half_float),
            pltpu.VMEM((STEPS, 2, ROWS, WIDE), half_float),
            pltpu.VMEM((STEPS, 2, N, WIDE), half_float),
            pltpu.VMEM((2, 2, T, 16, WIDE), half_float),
            pltpu.VMEM((2, 2, T, 16, WIDE), half_float),
            pltpu.VMEM((2 * T * 16, 128), single),
            pltpu.VMEM((2, 2, 8, 128, WIDE), half_float),
            pltpu.VMEM((4 * 128, 128), single),
            pltpu.VMEM((5, 256, 128), single),
            pltpu.VMEM((8, 8, 256), single),
            pltpu.VMEM((16, 8, 256), single),
            pltpu.VMEM((16, 8, 256), single),
            pltpu.VMEM((8, 256), single),
            pltpu.VMEM((8, 256), single),
            DMA((2,)), DMA, DMA,
        ]
        + [DMA((STEPS,))] * 8
        + [DMA((2, 2))] * 2
        + [DMA((16,))] * 4,
        compiler_params=pltpu.CompilerParams(
            collective_id=offset, has_side_effects=True, vmem_limit_bytes=48 * MIB
        ),
    )(delta, pair, left, right)


AHEAD = {1: 0, 2: 0, 3: 1, 4: 0, 5: -2, 6: 0}
FIRST_ALONE = (1, 2, 3, 5, 6)


def on_device(fields_left, fields_right, delta, pair):
    left, right = fields_left[:, :, 0], fields_right[:, :, 0]
    branches = [functools.partial(fused, offset, AHEAD[offset]) for offset in range(1, DMAX)]
    sums = lax.switch(delta[0] + delta[1] - DMAX - 1, branches, delta, pair, left, right)
    shape = (1, 2, 2, 2, 2 * HALF)
    return sums[0, :48].reshape(shape), sums[1, :48].reshape(shape)


def solution(mesh):
    split = P(None, None, "tm", "mode", None)
    out = P("tm", None, None, None, None)
    return jax.shard_map(
        on_device, mesh=mesh, in_specs=(split, split, P(), P()), out_specs=(out, out), check_vma=False
    )
```
